32 devices in a mesh: cent: 4 (over y, core), pass: 8 (over z, x).
Axes of the slice: x: 2, y: 2, z: 4, core: 2. Of those that a mesh axis runs over, the one named last changes fastest.
Arguments:
- queries: float32 [32, 32, 128], P('cent'), may hold values from -0.6 to 0.6
- centroids: float32 [262144, 128], P(('cent', 'pass')), may hold values from -0.6 to 0.6
- bucket_weights: float32 [4, 128], replicated, may hold values from -0.6 to 0.6
- touched: int32 [8, 4096], replicated, may hold values from 0 to 262143, as said below
- token_codes: int32 [4096, 64], P('pass'), may hold values from 0 to 4095
- residual_bits: int32 [4096, 2048], P('pass'), may hold values from 0 to 255
- candidate_blocks: int32 [32, 8, 32], P('cent', 'pass'), may hold values from 0 to 31, as said below
- block_counts: int32 [32, 8], P('cent', 'pass'), may hold values from 12 to 32, as said below
Outputs:
- candidate_scores: float32 [32, 8, 512], P('cent', 'pass')
- top_scores: float32 [32, 32], P('cent')
The draws below stay inside these ranges and needn't reach their ends.
Inputs may be any that keep to these rules, and one draw needn't show every extreme that they name: For every shard p and range r < 32, touched[p, r*128 + t] for t < 128 are distinct ids from r*8192 to (r+1)*8192 - 1. `candidate_blocks`: the 32 block ids of one query on one shard are distinct; entries past the count are valid ids that are not live. `block_counts`: every query has exactly 32 live blocks on some shard.
All inputs are finite; a program needn't handle non-finite values.
Results may differ from the reference program's by a relative error of at most 0.0003.
Values sent between devices are 32-bit elements; how exact they have to be, the bound alone decides.
A program may use at most 192 MiB of HBM per device.

```python
import jax
import jax.numpy as jnp
from jax import lax

DIM = 128
NCENT = 262144
QT = 32
NQ = 32
PT = 64
BLK = 16
NBLK = 32
NB = 32
TPR = 128
KTOP = 32
U = 4096
N_PASS = 8
DEVICES = 32


def draw_touched(key, part):
    rows_dev = NCENT // DEVICES
    keys = jax.random.split(jax.random.fold_in(key, 11), N_PASS * DEVICES)

    def pick_rows(sub_key):
        return jax.random.permutation(sub_key, rows_dev)[:TPR].astype(jnp.int32)
    picks = jax.vmap(pick_rows)(keys)
    base = jnp.arange(N_PASS * DEVICES, dtype=jnp.int32) % DEVICES * rows_dev
    return (picks + base[:, None]).reshape(N_PASS, DEVICES * TPR).astype(jnp.int32)


def draw_candidate_blocks(key, part):
    keys = jax.random.split(jax.random.fold_in(key, 23), NQ * N_PASS)

    def pick_blocks(sub_key):
        return jax.random.permutation(sub_key, NBLK)[:NB].astype(jnp.int32)
    return jax.vmap(pick_blocks)(keys).reshape(NQ, N_PASS, NB).astype(jnp.int32)


def draw_block_counts(key, part):
    first_key, second_key = jax.random.split(jax.random.fold_in(key, 37))
    least = max(1, 3 * NB // 8)
    light = jax.random.randint(first_key, (NQ, N_PASS), least, NB + 1).astype(jnp.int32)
    heavy = jax.random.randint(second_key, (NQ,), 0, N_PASS).astype(jnp.int32)
    chosen = jnp.arange(N_PASS, dtype=jnp.int32)[None, :] == heavy[:, None]
    return jnp.where(chosen, jnp.int32(NB), light).astype(jnp.int32)


def with_ends(array, own_key, low, top_value):
    dims = array.shape
    index_at = [jax.random.randint(jax.random.fold_in(own_key, axis), (), 0, dims[axis]) for axis in range(len(dims))]
    array = array.at[tuple(index_at)].set(low)
    longest = dims.index(max(dims))
    index_at[longest] = (index_at[longest] + 1) % dims[longest]
    return array.at[tuple(index_at)].set(top_value)


def block_levels(stream_key, shape, shards, low, largest):
    def one(position, blocks):
        heights = jax.random.uniform(jax.random.fold_in(jax.random.fold_in(stream_key, 6), position), (blocks,), jnp.float32, low / len(shards), largest / len(shards))
        return jnp.repeat(jnp.exp(heights), shape[position] // blocks).reshape((-1,) + (1,) * (len(shape) - position - 1))

    factor_of = one(*shards[0])
    for cut in shards[1:]:
        factor_of = factor_of * one(*cut)
    return factor_of


def bell_draw(key, shape, scale, limit, cuts=(), kind=jnp.bfloat16):
    array = jax.random.normal(key, shape, jnp.float32) * scale
    if len(cuts) > 0:
        array = block_levels(key, shape, cuts, -0.22, 0.18) * array
    return jnp.clip(array, min=-limit, max=limit).astype(kind)


def setup_inputs(seed: int = 0) -> dict:
    key_list = jax.random.split(jax.random.key(seed), 9)
    return {
        "queries": bell_draw(key_list[0], (NQ, QT, DIM), 0.0884, 0.6, ((0, 4),), jnp.float32),
        "centroids": bell_draw(key_list[1], (NCENT, DIM), 0.0884, 0.6, ((0, 32),), jnp.float32),
        "bucket_weights": bell_draw(key_list[2], (4, DIM), 0.1, 0.6, (), jnp.float32),
        "touched": draw_touched(jax.random.fold_in(key_list[8], 71), 0),
        "token_codes": with_ends(jax.random.randint(key_list[4], (NBLK * BLK * N_PASS, PT), 0, U), jax.random.fold_in(key_list[4], 1), 0, U - 1).astype(jnp.int32),
        "residual_bits": with_ends(jax.random.randint(key_list[5], (NBLK * BLK * N_PASS, PT * DIM // 4), 0, 256), jax.random.fold_in(key_list[5], 1), 0, 255).astype(jnp.int32),
        "candidate_blocks": draw_candidate_blocks(jax.random.fold_in(key_list[8], 71), 0),
        "block_counts": draw_block_counts(jax.random.fold_in(key_list[8], 71), 0),
    }


floor_value = -1.0e30


def score_queries(queries, table, shard_codes, shard_bits, bucket_weights, blocks, live_counts):
    query_count, query_len, width = queries.shape
    block_count = blocks.shape[1]
    passage_len = shard_codes.shape[1]
    word_count = shard_bits.shape[1] // passage_len
    slot_count = block_count * BLK
    shifts = 2 * jnp.arange(4, dtype=jnp.int32)

    def one_query(index):
        block_ids = lax.dynamic_index_in_dim(blocks, index, 0, keepdims=False)
        passage_rows = (block_ids[:, None] * BLK + jnp.arange(BLK, dtype=jnp.int32)[None, :]).reshape(-1)
        local_codes = jnp.take(shard_codes, passage_rows, axis=0).reshape(-1)
        packed = jnp.take(shard_bits, passage_rows, axis=0).reshape(-1, word_count)
        levels = jnp.bitwise_and(jnp.right_shift(packed[:, :, None], shifts[None, None, :]), 3).reshape(-1, width)
        residual = jnp.where(levels == 0, bucket_weights[0], jnp.where(levels == 1, bucket_weights[1], jnp.where(levels == 2, bucket_weights[2], bucket_weights[3])))
        query_rows = lax.dynamic_index_in_dim(queries, index, 0, keepdims=False)
        table_rows = lax.dynamic_slice_in_dim(table, index * query_len, query_len, 0)
        looked = jnp.take(table_rows, local_codes, axis=1)
        token_scores = looked + jnp.dot(query_rows, residual.T, precision=lax.Precision.HIGHEST)
        best = jnp.sum(jnp.max(token_scores.reshape(query_len, slot_count, passage_len), axis=2), axis=0)
        live = lax.dynamic_index_in_dim(live_counts, index, 0, keepdims=False)
        valid = (jnp.arange(slot_count, dtype=jnp.int32) // BLK) < live
        return jnp.where(valid, best, jnp.zeros((), jnp.float32)), jnp.where(valid, best, jnp.full((), floor_value, jnp.float32))

    return lax.map(one_query, jnp.arange(query_count, dtype=jnp.int32))


def reference(queries, centroids, bucket_weights, touched, token_codes, residual_bits, candidate_blocks, block_counts):
    query_count, query_len, width = queries.shape
    shard_count = touched.shape[0]
    shard_rows = token_codes.shape[0] // shard_count
    flat_queries = queries.reshape(query_count * query_len, width)

    def per_shard(shard):
        ids = lax.dynamic_index_in_dim(touched, shard, 0, keepdims=False)
        picked = jnp.take(centroids, ids, axis=0)
        table = jnp.dot(flat_queries, picked.T, precision=lax.Precision.HIGHEST)
        shard_codes = lax.dynamic_slice_in_dim(token_codes, shard * shard_rows, shard_rows, 0)
        shard_bits = lax.dynamic_slice_in_dim(residual_bits, shard * shard_rows, shard_rows, 0)
        blocks = lax.dynamic_index_in_dim(candidate_blocks, shard, 1, keepdims=False)
        live_counts = lax.dynamic_index_in_dim(block_counts, shard, 1, keepdims=False)
        return score_queries(queries, table, shard_codes, shard_bits, bucket_weights, blocks, live_counts)

    plain, masked = lax.map(per_shard, jnp.arange(shard_count, dtype=jnp.int32))
    candidate_scores = jnp.transpose(plain, (1, 0, 2))
    masked_all = jnp.transpose(masked, (1, 0, 2)).reshape(query_count, -1)
    top_scores = lax.top_k(masked_all, KTOP)[0]
    return candidate_scores, top_scores
```

```python
import functools

import jax
import jax.numpy as jnp
from jax import lax
from jax.experimental import pallas as pl
from jax.experimental.pallas import tpu as pltpu
from jax.sharding import PartitionSpec as P

BLK = 16
KTOP = 32
CHUNK = 16

floor_value = -1e30


def pick_kernel(count, wanted_ref, rows_ref, out_ref):
    def some(step, carry):
        base = pl.multiple_of(step * 16, 16)
        for k in range(16):
            row = wanted_ref[base + k]
            out_ref[pl.ds(base + k, 1), :] = rows_ref[pl.ds(row, 1), :]
        return carry

    lax.fori_loop(0, count // 16, some, 0)


def pick_rows(centroids, wanted):
    count = wanted.shape[0]
    width = centroids.shape[1]
    return pl.pallas_call(
        functools.partial(pick_kernel, count),
        out_shape=jax.ShapeDtypeStruct((count, width), jnp.float32),
        in_specs=[
            pl.BlockSpec(memory_space=pltpu.SMEM),
            pl.BlockSpec(memory_space=pltpu.VMEM),
        ],
        out_specs=pl.BlockSpec(memory_space=pltpu.VMEM),
        compiler_params=pltpu.CompilerParams(vmem_limit_bytes=24 * 2**20),
    )(wanted, centroids)


def score_kernel(
    passage_len, where_ref, codes_ref, bits_ref, weights_ref, query_ref, fold_ref, table_ref, out_ref, held
):
    chunk = pl.program_id(0)
    width = weights_ref.shape[1]
    rows = passage_len * CHUNK
    words = width // 4
    per_tile = width // words

    def some(step, carry):
        base = pl.multiple_of(step * CHUNK, CHUNK)
        for k in range(CHUNK):
            code = codes_ref[chunk * rows + base + k]
            held[pl.ds(base + k, 1), :] = table_ref[pl.ds(code, 1), :]
        return carry

    lax.fori_loop(0, passage_len, some, 0, unroll=4)

    tiles = passage_len // per_tile
    packed = jnp.concatenate(
        [bits_ref[:, i * width : (i + 1) * width] for i in range(tiles)], axis=0
    )
    source = lax.broadcasted_iota(jnp.int32, (width, width * per_tile), 0)
    target = lax.broadcasted_iota(jnp.int32, (width, width * per_tile), 1)
    spread = jnp.where(target // 4 == source, 1.0, 0.0).astype(jnp.bfloat16)
    wide = jnp.dot(
        packed.astype(jnp.float32).astype(jnp.bfloat16), spread, preferred_element_type=jnp.float32
    ).astype(jnp.int32)
    shift = 2 * (lax.broadcasted_iota(jnp.int32, (1, width), 1) % 4)
    parts = []
    for a in range(per_tile):
        level = jnp.right_shift(wide[:, a * width : (a + 1) * width], shift) & 3
        value = jnp.where(
            level == 0,
            weights_ref[0:1, :],
            jnp.where(
                level == 1,
                weights_ref[1:2, :],
                jnp.where(level == 2, weights_ref[2:3, :], weights_ref[3:4, :]),
            ),
        )
        parts.append(value.reshape(tiles, 1, CHUNK, width))
    residual = jnp.concatenate(parts, axis=1).reshape(rows, width)
    token = (held[...] + residual).astype(jnp.bfloat16)
    token = jnp.concatenate([token, token], axis=1)
    score = jnp.dot(token, query_ref[...], preferred_element_type=jnp.float32)
    best = jnp.max(score.reshape(passage_len, CHUNK, score.shape[1]), axis=0)
    out_ref[...] = lax.dot_general(
        best,
        fold_ref[...],
        (((1,), (0,)), ((), ())),
        precision=lax.Precision.HIGHEST,
        preferred_element_type=jnp.float32,
    )


def score_passages(all_queries, table, codes, bits, weights, where, mine):
    query_count, query_len, width = all_queries.shape
    passage_len = codes.shape[0] // mine
    flat = all_queries.reshape(query_count * query_len, width)
    high = lax.reduce_precision(flat, 8, 7)
    both = jnp.concatenate([high, flat - high], axis=1).T.astype(jnp.bfloat16)
    fold = (
        jnp.arange(query_count * query_len)[:, None] // query_len == jnp.arange(query_count)[None, :]
    ).astype(jnp.float32)
    chunks = mine // CHUNK
    whole = pl.Buffered(buffer_count=1)
    return pl.pallas_call(
        functools.partial(score_kernel, passage_len),
        out_shape=jax.ShapeDtypeStruct((mine, query_count), jnp.float32),
        grid_spec=pltpu.PrefetchScalarGridSpec(
            num_scalar_prefetch=2,
            grid=(chunks,),
            in_specs=[
                pl.BlockSpec((CHUNK, bits.shape[1]), lambda c, w, k: (w[0] * chunks + c, 0)),
                pl.BlockSpec(weights.shape, lambda c, w, k: (0, 0)),
                pl.BlockSpec(both.shape, lambda c, w, k: (0, 0), pipeline_mode=whole),
                pl.BlockSpec(fold.shape, lambda c, w, k: (0, 0), pipeline_mode=whole),
                pl.BlockSpec(table.shape, lambda c, w, k: (0, 0), pipeline_mode=whole),
            ],
            out_specs=pl.BlockSpec((CHUNK, query_count), lambda c, w, k: (c, 0)),
            scratch_shapes=[pltpu.VMEM((passage_len * CHUNK, width), jnp.float32)],
        ),
        compiler_params=pltpu.CompilerParams(vmem_limit_bytes=48 * 2**20),
    )(where, codes, bits, weights, both, fold, table)


def largest(values, keep):
    count = values.shape[1]
    place = jnp.arange(count, dtype=jnp.int32)
    one, other = values[:, :, None], values[:, None, :]
    ahead = (other > one) | ((other == one) & (place[None, None, :] < place[None, :, None]))
    rank = jnp.sum(ahead.astype(jnp.int32), axis=2)
    hit = rank[:, None, :] == jnp.arange(keep, dtype=jnp.int32)[None, :, None]
    return jnp.sum(jnp.where(hit, values[:, None, :], 0.0), axis=2)


def body(
    queries,
    centroids,
    bucket_weights,
    touched,
    token_codes,
    residual_bits,
    candidate_blocks,
    block_counts,
):
    group_queries, query_len, width = queries.shape
    pass_count = lax.axis_size("pass")
    cent_count = lax.axis_size("cent")
    row_count = centroids.shape[0]
    cent = lax.axis_index("cent").astype(jnp.int32)
    per_range = touched.shape[1] // (pass_count * cent_count)
    owner = cent * pass_count + lax.axis_index("pass")
    wanted = lax.dynamic_slice_in_dim(touched, owner * per_range, per_range, 1) - owner * row_count
    picked = pick_rows(centroids, wanted.reshape(-1))
    all_queries = lax.all_gather(queries, "cent", axis=0, tiled=True)
    arrived = lax.all_to_all(
        picked.reshape(pass_count, per_range, width), "pass", split_axis=0, concat_axis=0, tiled=True
    )
    table = lax.all_gather(arrived, "cent", axis=0, tiled=True).reshape(-1, width)

    passages, passage_len = token_codes.shape
    mine = passages // cent_count
    codes = lax.dynamic_slice_in_dim(token_codes, cent * mine, mine, 0)
    codes = codes.reshape(mine // CHUNK, CHUNK, passage_len).transpose(0, 2, 1).reshape(-1)
    scored = score_passages(
        all_queries, table, codes, residual_bits, bucket_weights, cent.reshape(1), mine
    )
    every = lax.all_to_all(scored.T, "cent", split_axis=0, concat_axis=1, tiled=True)

    blocks = candidate_blocks[:, 0, :]
    block_count = blocks.shape[1]
    stored = passages // BLK
    by_block = every.reshape(group_queries, 1, stored, BLK)
    chosen = blocks[:, :, None, None] == jnp.arange(stored, dtype=jnp.int32)[None, None, :, None]
    slots = jnp.sum(jnp.where(chosen, by_block, 0.0), axis=2)
    live = jnp.arange(block_count, dtype=jnp.int32)[None, :, None] < block_counts[:, :, None]
    plain = jnp.where(live, slots, 0.0).reshape(group_queries, -1)
    masked = jnp.where(live, slots, floor_value).reshape(group_queries, -1)
    local_top = largest(masked, KTOP)
    every_top = lax.all_gather(local_top, "pass", axis=1, tiled=True)
    return plain[:, None, :], largest(every_top, KTOP)


def solution(mesh):
    placed = (
        P("cent", None, None),
        P(("cent", "pass"), None),
        P(),
        P(),
        P("pass", None),
        P("pass", None),
        P("cent", "pass", None),
        P("cent", "pass"),
    )
    return jax.shard_map(
        body,
        mesh=mesh,
        in_specs=placed,
        out_specs=(P("cent", "pass", None), P("cent", None)),
        check_vma=False,
    )
```

```python
import functools

import jax
import jax.numpy as jnp
from jax import lax
from jax.experimental import pallas as pl
from jax.experimental.pallas import tpu as pltpu
from jax.sharding import PartitionSpec as P

BLK = 16
KTOP = 32
CHUNK = 16

floor_value = -1e30


MESH = pl.DeviceIdType.MESH


def meet(peers):
    barrier = pltpu.get_barrier_semaphore()
    for peer in peers:
        pl.semaphore_signal(barrier, inc=1, device_id=peer, device_id_type=MESH)
    pl.semaphore_wait(barrier, len(peers))


def spread_kernel(
    pass_count,
    cent_count,
    per_range,
    wanted_ref,
    rows_ref,
    queries_ref,
    table_ref,
    all_ref,
    picked,
    out_sem,
    in_sem,
    query_out_sem,
    query_in_sem,
):
    cent, own = lax.axis_index("cent"), lax.axis_index("pass")
    core, pair = cent % 2, cent // 2
    pairs = cent_count // 2
    twin = (cent + 1 - 2 * core, own)
    sides = [((pair + s) % pairs * 2 + core, own) for s in range(1, pairs)]
    meet([(cent, (own + s) % pass_count) for s in range(1, pass_count)] + sides + [twin])

    def send_query(slot, peer, source=None):
        pltpu.make_async_remote_copy(
            src_ref=all_ref.at[slot] if source is None else source,
            dst_ref=all_ref.at[slot],
            send_sem=query_out_sem,
            recv_sem=query_in_sem.at[slot],
            device_id=peer,
            device_id_type=MESH,
        ).start()

    def send(source, slot, peer):
        pltpu.make_async_remote_copy(
            src_ref=source,
            dst_ref=table_ref.at[slot],
            send_sem=out_sem,
            recv_sem=in_sem.at[slot],
            device_id=peer,
            device_id_type=MESH,
        ).start()

    def arrived(slot):
        pltpu.make_async_copy(table_ref.at[slot], table_ref.at[slot], in_sem.at[slot]).wait()

    def query_arrived(slot):
        pltpu.make_async_copy(all_ref.at[slot], all_ref.at[slot], query_in_sem.at[slot]).wait()

    def pick(target):
        def some(step, carry):
            base = pl.multiple_of(step * 16, 16)
            for k in range(16):
                row = wanted_ref[target * per_range + base + k]
                picked[target, pl.ds(base + k, 1), :] = rows_ref[pl.ds(row, 1), :]
            return carry

        lax.fori_loop(0, per_range // 16, some, 0)

    def give(step, carry):
        target = (own + step) % pass_count
        pick(target)
        send(picked.at[target], cent * pass_count + own, (cent, target))
        return carry

    lax.fori_loop(1, pass_count, give, 0)
    all_ref[cent] = queries_ref[...]
    for side in sides:
        send_query(cent, side)
    send_query(cent, twin)
    pick(own)
    table_ref[cent * pass_count + own] = picked[own]

    def forward(slot):
        for side in sides:
            send(table_ref.at[slot], slot, side)
        send(table_ref.at[slot], slot, twin)

    forward(cent * pass_count + own)

    def take(step, carry):
        slot = cent * pass_count + (own + pass_count - step) % pass_count
        arrived(slot)
        forward(slot)
        return carry

    lax.fori_loop(1, pass_count, take, 0)
    for s in range(1, pairs):
        other = (pair + pairs - s) % pairs * 2 + core
        query_arrived(other)
        send_query(other, twin)

        def cross(step, carry):
            slot = other * pass_count + (own + pass_count - step) % pass_count
            arrived(slot)
            send(table_ref.at[slot], slot, twin)
            return carry

        lax.fori_loop(0, pass_count, cross, 0)

    for k in range(pairs):
        other = k * 2 + 1 - core
        query_arrived(other)

        def last(step, carry):
            arrived(other * pass_count + step)
            return carry

        lax.fori_loop(0, pass_count, last, 0)
    sent = table_ref.at[pl.ds(0, cent_count * pass_count - 1)]
    pltpu.make_async_copy(sent, sent, out_sem).wait()
    sent = all_ref.at[pl.ds(0, cent_count - 1)]
    pltpu.make_async_copy(sent, sent, query_out_sem).wait()


def spread_rows(queries, centroids, wanted, cent_count, pass_count):
    per_range = wanted.shape[0] // pass_count
    width = centroids.shape[1]
    slots = cent_count * pass_count
    return pl.pallas_call(
        functools.partial(spread_kernel, pass_count, cent_count, per_range),
        out_shape=(
            jax.ShapeDtypeStruct((slots, per_range, width), jnp.float32),
            jax.ShapeDtypeStruct((cent_count,) + queries.shape, jnp.float32),
        ),
        in_specs=[
            pl.BlockSpec(memory_space=pltpu.SMEM),
            pl.BlockSpec(memory_space=pltpu.VMEM),
            pl.BlockSpec(memory_space=pltpu.VMEM),
        ],
        out_specs=(pl.BlockSpec(memory_space=pltpu.VMEM), pl.BlockSpec(memory_space=pltpu.VMEM)),
        scratch_shapes=[
            pltpu.VMEM((pass_count, per_range, width), jnp.float32),
            pltpu.SemaphoreType.DMA,
            pltpu.SemaphoreType.DMA((slots,)),
            pltpu.SemaphoreType.DMA,
            pltpu.SemaphoreType.DMA((cent_count,)),
        ],
        compiler_params=pltpu.CompilerParams(
            collective_id=0, has_side_effects=True, vmem_limit_bytes=40 * 2**20
        ),
    )(wanted, centroids, queries)


def finish_kernel(
    pass_count, cent_count, keep, part_ref, mask_ref, every_ref, top_ref, box, out_sem, in_sem, box_out_sem, box_in_sem
):
    cent, own = lax.axis_index("cent"), lax.axis_index("pass")
    group = part_ref.shape[1]
    across = [(cent + s) % cent_count for s in range(1, cent_count)]
    along = [(own + s) % pass_count for s in range(1, pass_count)]
    meet([(c, own) for c in across] + [(cent, p) for p in along])
    copies = []
    for k, c in enumerate(across):
        copy = pltpu.make_async_remote_copy(
            src_ref=part_ref.at[c],
            dst_ref=every_ref.at[cent],
            send_sem=out_sem.at[k],
            recv_sem=in_sem.at[k],
            device_id=(c, own),
            device_id_type=MESH,
        )
        copy.start()
        copies.append(copy)
    every_ref[cent] = part_ref[cent]
    for copy in copies:
        copy.wait()
    box[own] = jnp.where(mask_ref[...] > 0, every_ref[...], floor_value)
    copies = []
    for k, p in enumerate(along):
        copy = pltpu.make_async_remote_copy(
            src_ref=box.at[own],
            dst_ref=box.at[own],
            send_sem=box_out_sem.at[k],
            recv_sem=box_in_sem.at[k],
            device_id=(cent, p),
            device_id_type=MESH,
        )
        copy.start()
        copies.append(copy)
    for copy in copies:
        copy.wait()
    place = lax.broadcasted_iota(jnp.int32, (group, keep), 1).astype(jnp.float32)

    def step(i, carry):
        bound, done, top = carry
        x = box[...]
        x = x.reshape((pass_count * cent_count,) + x.shape[2:])
        lower = jnp.max(jnp.where(x < bound, x, -jnp.inf), axis=0)
        value = jnp.max(lower, axis=1, keepdims=True)
        same = jnp.sum(jnp.where(x == value, 1.0, 0.0), axis=0)
        after = done + jnp.sum(same, axis=1, keepdims=True)
        top = jnp.where((place >= done) & (place < after), value, top)
        return value, after, top

    first = (
        jnp.full((group, 1), jnp.inf, jnp.float32),
        jnp.zeros((group, 1), jnp.float32),
        jnp.zeros((group, keep), jnp.float32),
    )
    top_ref[...] = lax.fori_loop(0, keep, step, first)[2]


def finish(parts, mask, pass_count):
    cent_count, group, mine = parts.shape
    return pl.pallas_call(
        functools.partial(finish_kernel, pass_count, cent_count, KTOP),
        out_shape=(
            jax.ShapeDtypeStruct(parts.shape, jnp.float32),
            jax.ShapeDtypeStruct((group, KTOP), jnp.float32),
        ),
        in_specs=[pl.BlockSpec(memory_space=pltpu.VMEM)] * 2,
        out_specs=(pl.BlockSpec(memory_space=pltpu.VMEM), pl.BlockSpec(memory_space=pltpu.VMEM)),
        scratch_shapes=[
            pltpu.VMEM((pass_count, cent_count, group, mine), jnp.float32),
            pltpu.SemaphoreType.DMA((cent_count,)),
            pltpu.SemaphoreType.DMA((cent_count,)),
            pltpu.SemaphoreType.DMA((pass_count,)),
            pltpu.SemaphoreType.DMA((pass_count,)),
        ],
        compiler_params=pltpu.CompilerParams(collective_id=1, has_side_effects=True),
    )(parts, mask)


def score_kernel(
    passage_len, where_ref, codes_ref, bits_ref, weights_ref, query_ref, fold_ref, table_ref, out_ref, held
):
    chunk = pl.program_id(0)
    width = weights_ref.shape[1]
    rows = passage_len * CHUNK
    words = width // 4
    per_tile = width // words

    def some(step, carry):
        base = pl.multiple_of(step * CHUNK, CHUNK)
        for k in range(CHUNK):
            code = codes_ref[chunk * rows + base + k]
            held[pl.ds(base + k, 1), :] = table_ref[pl.ds(code, 1), :]
        return carry

    lax.fori_loop(0, passage_len, some, 0, unroll=4)

    tiles = passage_len // per_tile
    packed = jnp.concatenate(
        [bits_ref[:, i * width : (i + 1) * width] for i in range(tiles)], axis=0
    )
    source = lax.broadcasted_iota(jnp.int32, (width, width * per_tile), 0)
    target = lax.broadcasted_iota(jnp.int32, (width, width * per_tile), 1)
    spread = jnp.where(target // 4 == source, 1.0, 0.0).astype(jnp.bfloat16)
    wide = jnp.dot(
        packed.astype(jnp.float32).astype(jnp.bfloat16), spread, preferred_element_type=jnp.float32
    ).astype(jnp.int32)
    shift = 2 * (lax.broadcasted_iota(jnp.int32, (1, width), 1) % 4)
    parts = []
    for a in range(per_tile):
        level = jnp.right_shift(wide[:, a * width : (a + 1) * width], shift) & 3
        value = jnp.where(
            level == 0,
            weights_ref[0:1, :],
            jnp.where(
                level == 1,
                weights_ref[1:2, :],
                jnp.where(level == 2, weights_ref[2:3, :], weights_ref[3:4, :]),
            ),
        )
        parts.append(value.reshape(tiles, 1, CHUNK, width))
    residual = jnp.concatenate(parts, axis=1).reshape(rows, width)
    token = (held[...] + residual).astype(jnp.bfloat16)
    token = jnp.concatenate([token, token], axis=1)
    score = jnp.dot(token, query_ref[...], preferred_element_type=jnp.float32)
    best = jnp.max(score.reshape(passage_len, CHUNK, score.shape[1]), axis=0)
    out_ref[...] = lax.dot_general(
        best,
        fold_ref[...],
        (((1,), (0,)), ((), ())),
        precision=lax.Precision.HIGHEST,
        preferred_element_type=jnp.float32,
    )


def score_passages(all_queries, table, codes, bits, weights, where, mine):
    query_count, query_len, width = all_queries.shape
    passage_len = codes.shape[0] // mine
    flat = all_queries.reshape(query_count * query_len, width)
    high = lax.reduce_precision(flat, 8, 7)
    both = jnp.concatenate([high, flat - high], axis=1).T.astype(jnp.bfloat16)
    fold = (
        jnp.arange(query_count * query_len)[:, None] // query_len == jnp.arange(query_count)[None, :]
    ).astype(jnp.float32)
    chunks = mine // CHUNK
    whole = pl.Buffered(buffer_count=1)
    return pl.pallas_call(
        functools.partial(score_kernel, passage_len),
        out_shape=jax.ShapeDtypeStruct((mine, query_count), jnp.float32),
        grid_spec=pltpu.PrefetchScalarGridSpec(
            num_scalar_prefetch=2,
            grid=(chunks,),
            in_specs=[
                pl.BlockSpec((CHUNK, bits.shape[1]), lambda c, w, k: (w[0] * chunks + c, 0)),
                pl.BlockSpec(weights.shape, lambda c, w, k: (0, 0)),
                pl.BlockSpec(both.shape, lambda c, w, k: (0, 0), pipeline_mode=whole),
                pl.BlockSpec(fold.shape, lambda c, w, k: (0, 0), pipeline_mode=whole),
                pl.BlockSpec(table.shape, lambda c, w, k: (0, 0), pipeline_mode=whole),
            ],
            out_specs=pl.BlockSpec((CHUNK, query_count), lambda c, w, k: (c, 0)),
            scratch_shapes=[pltpu.VMEM((passage_len * CHUNK, width), jnp.float32)],
        ),
        compiler_params=pltpu.CompilerParams(vmem_limit_bytes=48 * 2**20),
    )(where, codes, bits, weights, both, fold, table)


def body(
    queries,
    centroids,
    bucket_weights,
    touched,
    token_codes,
    residual_bits,
    candidate_blocks,
    block_counts,
):
    group_queries, query_len, width = queries.shape
    pass_count = lax.axis_size("pass")
    cent_count = lax.axis_size("cent")
    row_count = centroids.shape[0]
    cent = lax.axis_index("cent").astype(jnp.int32)
    per_range = touched.shape[1] // (pass_count * cent_count)
    owner = cent * pass_count + lax.axis_index("pass")
    wanted = lax.dynamic_slice_in_dim(touched, owner * per_range, per_range, 1) - owner * row_count
    table, all_queries = spread_rows(queries, centroids, wanted.reshape(-1), cent_count, pass_count)
    table = table.reshape(-1, width)
    all_queries = all_queries.reshape(-1, query_len, width)

    passages, passage_len = token_codes.shape
    mine = passages // cent_count
    codes = lax.dynamic_slice_in_dim(token_codes, cent * mine, mine, 0)
    codes = codes.reshape(mine // CHUNK, CHUNK, passage_len).transpose(0, 2, 1).reshape(-1)
    scored = score_passages(
        all_queries, table, codes, residual_bits, bucket_weights, cent.reshape(1), mine
    )

    blocks = candidate_blocks[:, 0, :]
    block_count = blocks.shape[1]
    stored = passages // BLK
    live = jnp.arange(block_count, dtype=jnp.int32)[None, :] < block_counts
    holds = blocks[:, :, None] == jnp.arange(stored, dtype=jnp.int32)[None, None, :]
    wanted_blocks = jnp.any(holds & live[:, :, None], axis=1).astype(jnp.int32)
    mask = jnp.repeat(wanted_blocks, BLK, axis=1).reshape(group_queries, cent_count, mine)
    parts = scored.T.reshape(cent_count, group_queries, mine)
    every, top = finish(parts, mask.transpose(1, 0, 2), pass_count)
    by_block = every.transpose(1, 0, 2).reshape(group_queries, 1, stored, BLK)
    slots = jnp.sum(jnp.where(holds[:, :, :, None], by_block, 0.0), axis=2)
    plain = jnp.where(live[:, :, None], slots, 0.0).reshape(group_queries, -1)
    return plain[:, None, :], top


def solution(mesh):
    placed = (
        P("cent", None, None),
        P(("cent", "pass"), None),
        P(),
        P(),
        P("pass", None),
        P("pass", None),
        P("cent", "pass", None),
        P("cent", "pass"),
    )
    return jax.shard_map(
        body,
        mesh=mesh,
        in_specs=placed,
        out_specs=(P("cent", "pass", None), P("cent", None)),
        check_vma=False,
    )
```

```python
import functools

import jax
import jax.numpy as jnp
from jax import lax
from jax.experimental import pallas as pl
from jax.experimental.pallas import tpu as pltpu
from jax.sharding import PartitionSpec as P

BLK = 16
KTOP = 32
CHUNK = 16

floor_value = -1e30


MESH = pl.DeviceIdType.MESH


def meet(peers):
    barrier = pltpu.get_barrier_semaphore()
    for peer in peers:
        pl.semaphore_signal(barrier, inc=1, device_id=peer, device_id_type=MESH)
    pl.semaphore_wait(barrier, len(peers))


def spread_kernel(
    pass_count,
    cent_count,
    per_range,
    wanted_ref,
    rows_ref,
    queries_ref,
    table_ref,
    all_ref,
    picked,
    out_sem,
    in_sem,
    query_out_sem,
    query_in_sem,
):
    cent, own = lax.axis_index("cent"), lax.axis_index("pass")
    core, pair = cent % 2, cent // 2
    pairs = cent_count // 2
    twin = (cent + 1 - 2 * core, own)
    sides = [((pair + s) % pairs * 2 + core, own) for s in range(1, pairs)]
    meet([(cent, (own + s) % pass_count) for s in range(1, pass_count)] + sides + [twin])

    def send_query(slot, peer, source=None):
        pltpu.make_async_remote_copy(
            src_ref=all_ref.at[slot] if source is None else source,
            dst_ref=all_ref.at[slot],
            send_sem=query_out_sem,
            recv_sem=query_in_sem.at[slot],
            device_id=peer,
            device_id_type=MESH,
        ).start()

    def send(source, slot, peer):
        pltpu.make_async_remote_copy(
            src_ref=source,
            dst_ref=table_ref.at[slot],
            send_sem=out_sem,
            recv_sem=in_sem.at[slot],
            device_id=peer,
            device_id_type=MESH,
        ).start()

    def arrived(slot):
        pltpu.make_async_copy(table_ref.at[slot], table_ref.at[slot], in_sem.at[slot]).wait()

    def query_arrived(slot):
        pltpu.make_async_copy(all_ref.at[slot], all_ref.at[slot], query_in_sem.at[slot]).wait()

    def pick(target):
        def some(step, carry):
            base = pl.multiple_of(step * 16, 16)
            for k in range(16):
                row = wanted_ref[target * per_range + base + k]
                picked[target, pl.ds(base + k, 1), :] = rows_ref[pl.ds(row, 1), :]
            return carry

        lax.fori_loop(0, per_range // 16, some, 0)

    def give(step, carry):
        target = (own + step) % pass_count
        pick(target)
        send(picked.at[target], cent * pass_count + own, (cent, target))
        return carry

    lax.fori_loop(1, pass_count, give, 0)
    all_ref[cent] = queries_ref[...]
    for side in sides:
        send_query(cent, side)
    send_query(cent, twin)
    pick(own)
    table_ref[cent * pass_count + own] = picked[own]

    def forward(slot):
        for side in sides:
            send(table_ref.at[slot], slot, side)
        send(table_ref.at[slot], slot, twin)

    forward(cent * pass_count + own)

    def take(step, carry):
        slot = cent * pass_count + (own + pass_count - step) % pass_count
        arrived(slot)
        forward(slot)
        return carry

    lax.fori_loop(1, pass_count, take, 0)
    for s in range(1, pairs):
        other = (pair + pairs - s) % pairs * 2 + core
        query_arrived(other)
        send_query(other, twin)

        def cross(step, carry):
            slot = other * pass_count + (own + pass_count - step) % pass_count
            arrived(slot)
            send(table_ref.at[slot], slot, twin)
            return carry

        lax.fori_loop(0, pass_count, cross, 0)

    for k in range(pairs):
        other = k * 2 + 1 - core
        query_arrived(other)

        def last(step, carry):
            arrived(other * pass_count + step)
            return carry

        lax.fori_loop(0, pass_count, last, 0)
    sent = table_ref.at[pl.ds(0, cent_count * pass_count - 1)]
    pltpu.make_async_copy(sent, sent, out_sem).wait()
    sent = all_ref.at[pl.ds(0, cent_count - 1)]
    pltpu.make_async_copy(sent, sent, query_out_sem).wait()


def spread_rows(queries, centroids, wanted, cent_count, pass_count):
    per_range = wanted.shape[0] // pass_count
    width = centroids.shape[1]
    slots = cent_count * pass_count
    return pl.pallas_call(
        functools.partial(spread_kernel, pass_count, cent_count, per_range),
        out_shape=(
            jax.ShapeDtypeStruct((slots, per_range, width), jnp.float32),
            jax.ShapeDtypeStruct((cent_count,) + queries.shape, jnp.float32),
        ),
        in_specs=[
            pl.BlockSpec(memory_space=pltpu.SMEM),
            pl.BlockSpec(memory_space=pltpu.VMEM),
            pl.BlockSpec(memory_space=pltpu.VMEM),
        ],
        out_specs=(pl.BlockSpec(memory_space=pltpu.VMEM), pl.BlockSpec(memory_space=pltpu.VMEM)),
        scratch_shapes=[
            pltpu.VMEM((pass_count, per_range, width), jnp.float32),
            pltpu.SemaphoreType.DMA,
            pltpu.SemaphoreType.DMA((slots,)),
            pltpu.SemaphoreType.DMA,
            pltpu.SemaphoreType.DMA((cent_count,)),
        ],
        compiler_params=pltpu.CompilerParams(
            collective_id=0, has_side_effects=True, vmem_limit_bytes=40 * 2**20
        ),
    )(wanted, centroids, queries)


def finish_kernel(
    pass_count, cent_count, part_ref, mask_ref, every_ref, box, out_sem, in_sem, box_out_sem, box_in_sem
):
    cent, own = lax.axis_index("cent"), lax.axis_index("pass")
    across = [(cent + s) % cent_count for s in range(1, cent_count)]
    along = [(own + s) % pass_count for s in range(1, pass_count)]
    meet([(c, own) for c in across] + [(cent, p) for p in along])
    copies = []
    for k, c in enumerate(across):
        copy = pltpu.make_async_remote_copy(
            src_ref=part_ref.at[c],
            dst_ref=every_ref.at[cent],
            send_sem=out_sem.at[k],
            recv_sem=in_sem.at[k],
            device_id=(c, own),
            device_id_type=MESH,
        )
        copy.start()
        copies.append(copy)
    every_ref[cent] = part_ref[cent]
    for copy in copies:
        copy.wait()
    box[own] = jnp.where(mask_ref[...] > 0, every_ref[...], floor_value)
    copies = []
    for k, p in enumerate(along):
        copy = pltpu.make_async_remote_copy(
            src_ref=box.at[own],
            dst_ref=box.at[own],
            send_sem=box_out_sem.at[k],
            recv_sem=box_in_sem.at[k],
            device_id=(cent, p),
            device_id_type=MESH,
        )
        copy.start()
        copies.append(copy)
    for copy in copies:
        copy.wait()


def exchange(values, near, far):
    return jnp.maximum(values[near], values[far]), jnp.minimum(values[near], values[far])


def settle(values):
    gap = len(values) // 2
    while gap:
        for i in range(len(values)):
            if not i & gap:
                values[i], values[i + gap] = exchange(values, i, i + gap)
        gap //= 2
    return values


def descending(values):
    if len(values) == 1:
        return values
    half = len(values) // 2
    return settle(descending(values[:half]) + descending(values[half:])[::-1])


def merged(first, second):
    return settle([jnp.maximum(x, y) for x, y in zip(first, second[::-1])])


def top_kernel(keep, box_ref, top_ref):
    pass_count, cent_count, group, mine = box_ref.shape
    values = [box_ref[p, c] for p in range(pass_count) for c in range(cent_count)]
    runs = [descending(values[i : i + keep]) for i in range(0, len(values), keep)]
    best = runs[0]
    for run in runs[1:]:
        best = merged(best, run)
    gap = mine // 2
    while gap:
        if mine % 128 == 0:
            moved = [pltpu.roll(x, gap, 1) for x in best]
        else:
            moved = [jnp.concatenate([x[:, gap:], x[:, :gap]], axis=1) for x in best]
        best = merged(best, moved)
        gap //= 2
    place = lax.broadcasted_iota(jnp.int32, (group, mine), 1)
    out = best[0]
    for k in range(1, keep):
        out = jnp.where(place == k, best[k], out)
    top_ref[...] = out[:, :keep]


def largest(box):
    return pl.pallas_call(
        functools.partial(top_kernel, KTOP),
        out_shape=jax.ShapeDtypeStruct((box.shape[2], KTOP), jnp.float32),
        in_specs=[pl.BlockSpec(memory_space=pltpu.VMEM)],
        out_specs=pl.BlockSpec(memory_space=pltpu.VMEM),
    )(box)


def finish(parts, mask, pass_count):
    cent_count = parts.shape[0]
    return pl.pallas_call(
        functools.partial(finish_kernel, pass_count, cent_count),
        out_shape=(
            jax.ShapeDtypeStruct(parts.shape, jnp.float32),
            jax.ShapeDtypeStruct((pass_count,) + parts.shape, jnp.float32),
        ),
        in_specs=[pl.BlockSpec(memory_space=pltpu.VMEM)] * 2,
        out_specs=(pl.BlockSpec(memory_space=pltpu.VMEM), pl.BlockSpec(memory_space=pltpu.VMEM)),
        scratch_shapes=[
            pltpu.SemaphoreType.DMA((cent_count,)),
            pltpu.SemaphoreType.DMA((cent_count,)),
            pltpu.SemaphoreType.DMA((pass_count,)),
            pltpu.SemaphoreType.DMA((pass_count,)),
        ],
        compiler_params=pltpu.CompilerParams(collective_id=1, has_side_effects=True),
    )(parts, mask)


def score_kernel(
    passage_len, where_ref, codes_ref, bits_ref, weights_ref, query_ref, fold_ref, table_ref, out_ref, held, best
):
    chunk = pl.program_id(0)
    width = weights_ref.shape[1]
    rows = passage_len * CHUNK
    words = width // 4
    per_tile = width // words

    def some(step, carry):
        base = pl.multiple_of(step * CHUNK, CHUNK)
        for k in range(CHUNK):
            code = codes_ref[chunk * rows + base + k]
            held[pl.ds(base + k, 1), :] = table_ref[pl.ds(code, 1), :]
        return carry

    lax.fori_loop(0, passage_len, some, 0, unroll=4)

    tiles = passage_len // per_tile
    packed = jnp.concatenate(
        [bits_ref[:, i * width : (i + 1) * width] for i in range(tiles)], axis=0
    )
    source = lax.broadcasted_iota(jnp.int32, (width, width * per_tile), 0)
    target = lax.broadcasted_iota(jnp.int32, (width, width * per_tile), 1)
    spread = jnp.where(target // 4 == source, 1.0, 0.0).astype(jnp.bfloat16)
    wide = jnp.dot(
        packed.astype(jnp.float32).astype(jnp.bfloat16), spread, preferred_element_type=jnp.float32
    ).astype(jnp.int32)
    shift = 2 * (lax.broadcasted_iota(jnp.int32, (1, width), 1) % 4)
    parts = []
    for a in range(per_tile):
        level = jnp.right_shift(wide[:, a * width : (a + 1) * width], shift) & 3
        value = jnp.where(
            level == 0,
            weights_ref[0:1, :],
            jnp.where(
                level == 1,
                weights_ref[1:2, :],
                jnp.where(level == 2, weights_ref[2:3, :], weights_ref[3:4, :]),
            ),
        )
        parts.append(value.reshape(tiles, 1, CHUNK, width))
    residual = jnp.concatenate(parts, axis=1).reshape(rows, width)
    token = (held[...] + residual).astype(jnp.bfloat16)
    token = jnp.concatenate([token, token], axis=1)
    score = jnp.dot(token, query_ref[...], preferred_element_type=jnp.float32)
    peak = jnp.max(score.reshape(passage_len, CHUNK, score.shape[1]), axis=0)
    best[pl.ds(pl.multiple_of(chunk * CHUNK, CHUNK), CHUNK), :] = peak

    @pl.when(chunk == pl.num_programs(0) - 1)
    def _():
        out_ref[...] = lax.dot_general(
            fold_ref[...],
            best[...],
            (((1,), (1,)), ((), ())),
            precision=lax.Precision.HIGHEST,
            preferred_element_type=jnp.float32,
        )


def score_passages(all_queries, table, codes, bits, weights, where, mine):
    query_count, query_len, width = all_queries.shape
    passage_len = codes.shape[0] // mine
    flat = all_queries.reshape(query_count * query_len, width)
    high = lax.reduce_precision(flat, 8, 7)
    both = jnp.concatenate([high, flat - high], axis=1).T.astype(jnp.bfloat16)
    fold = (
        jnp.arange(query_count * query_len)[None, :] // query_len == jnp.arange(query_count)[:, None]
    ).astype(jnp.float32)
    chunks = mine // CHUNK
    whole = pl.Buffered(buffer_count=1)
    return pl.pallas_call(
        functools.partial(score_kernel, passage_len),
        out_shape=jax.ShapeDtypeStruct((query_count, mine), jnp.float32),
        grid_spec=pltpu.PrefetchScalarGridSpec(
            num_scalar_prefetch=2,
            grid=(chunks,),
            in_specs=[
                pl.BlockSpec((CHUNK, bits.shape[1]), lambda c, w, k: (w[0] * chunks + c, 0)),
                pl.BlockSpec(weights.shape, lambda c, w, k: (0, 0)),
                pl.BlockSpec(both.shape, lambda c, w, k: (0, 0), pipeline_mode=whole),
                pl.BlockSpec(fold.shape, lambda c, w, k: (0, 0), pipeline_mode=whole),
                pl.BlockSpec(table.shape, lambda c, w, k: (0, 0), pipeline_mode=whole),
            ],
            out_specs=pl.BlockSpec((query_count, mine), lambda c, w, k: (0, 0)),
            scratch_shapes=[
                pltpu.VMEM((passage_len * CHUNK, width), jnp.float32),
                pltpu.VMEM((mine, query_count * query_len), jnp.float32),
            ],
        ),
        compiler_params=pltpu.CompilerParams(vmem_limit_bytes=48 * 2**20),
    )(where, codes, bits, weights, both, fold, table)


def body(
    queries,
    centroids,
    bucket_weights,
    touched,
    token_codes,
    residual_bits,
    candidate_blocks,
    block_counts,
):
    group_queries, query_len, width = queries.shape
    pass_count = lax.axis_size("pass")
    cent_count = lax.axis_size("cent")
    row_count = centroids.shape[0]
    cent = lax.axis_index("cent").astype(jnp.int32)
    per_range = touched.shape[1] // (pass_count * cent_count)
    owner = cent * pass_count + lax.axis_index("pass")
    wanted = lax.dynamic_slice_in_dim(touched, owner * per_range, per_range, 1) - owner * row_count
    table, all_queries = spread_rows(queries, centroids, wanted.reshape(-1), cent_count, pass_count)
    table = table.reshape(-1, width)
    all_queries = all_queries.reshape(-1, query_len, width)

    passages, passage_len = token_codes.shape
    mine = passages // cent_count
    codes = lax.dynamic_slice_in_dim(token_codes, cent * mine, mine, 0)
    codes = codes.reshape(mine // CHUNK, CHUNK, passage_len).transpose(0, 2, 1).reshape(-1)
    scored = score_passages(
        all_queries, table, codes, residual_bits, bucket_weights, cent.reshape(1), mine
    )

    blocks = candidate_blocks[:, 0, :]
    block_count = blocks.shape[1]
    stored = passages // BLK
    live = jnp.arange(block_count, dtype=jnp.int32)[None, :] < block_counts
    holds = blocks[:, :, None] == jnp.arange(stored, dtype=jnp.int32)[None, None, :]
    wanted_blocks = jnp.any(holds & live[:, :, None], axis=1).astype(jnp.int32)
    mask = jnp.repeat(wanted_blocks, BLK, axis=1).reshape(group_queries, cent_count, mine)
    parts = scored.reshape(cent_count, group_queries, mine)
    every, box = finish(parts, mask.transpose(1, 0, 2), pass_count)
    by_block = every.transpose(1, 0, 2).reshape(group_queries, 1, stored, BLK)
    slots = jnp.sum(jnp.where(holds[:, :, :, None], by_block, 0.0), axis=2)
    plain = jnp.where(live[:, :, None], slots, 0.0).reshape(group_queries, -1)
    return plain[:, None, :], largest(box)


def solution(mesh):
    placed = (
        P("cent", None, None),
        P(("cent", "pass"), None),
        P(),
        P(),
        P("pass", None),
        P("pass", None),
        P("cent", "pass", None),
        P("cent", "pass"),
    )
    return jax.shard_map(
        body,
        mesh=mesh,
        in_specs=placed,
        out_specs=(P("cent", "pass", None), P("cent", None)),
        check_vma=False,
    )
```

```python
import functools

import jax
import jax.numpy as jnp
from jax import lax
from jax.experimental import pallas as pl
from jax.experimental.pallas import tpu as pltpu
from jax.sharding import PartitionSpec as P

BLK = 16
KTOP = 32
CHUNK = 16

floor_value = -1e30


MESH = pl.DeviceIdType.MESH


def meet(peers):
    barrier = pltpu.get_barrier_semaphore()
    for peer in peers:
        pl.semaphore_signal(barrier, inc=1, device_id=peer, device_id_type=MESH)
    pl.semaphore_wait(barrier, len(peers))


def spread_kernel(
    pass_count,
    cent_count,
    per_range,
    wanted_ref,
    stored_ref,
    queries_ref,
    table_ref,
    all_ref,
    rows_ref,
    picked,
    fetch_sem,
    out_sem,
    in_sem,
    query_out_sem,
    query_in_sem,
):
    cent, own = lax.axis_index("cent"), lax.axis_index("pass")
    core, pair = cent % 2, cent // 2
    pairs = cent_count // 2
    twin = (cent + 1 - 2 * core, own)
    sides = [((pair + s) % pairs * 2 + core, own) for s in range(1, pairs)]
    fetch = pltpu.make_async_copy(stored_ref, rows_ref, fetch_sem)
    fetch.start()
    meet([(cent, (own + s) % pass_count) for s in range(1, pass_count)] + sides + [twin])
    fetch.wait()

    def send_query(slot, peer, source=None):
        pltpu.make_async_remote_copy(
            src_ref=all_ref.at[slot] if source is None else source,
            dst_ref=all_ref.at[slot],
            send_sem=query_out_sem,
            recv_sem=query_in_sem.at[slot],
            device_id=peer,
            device_id_type=MESH,
        ).start()

    def send(source, slot, peer):
        pltpu.make_async_remote_copy(
            src_ref=source,
            dst_ref=table_ref.at[slot],
            send_sem=out_sem,
            recv_sem=in_sem.at[slot],
            device_id=peer,
            device_id_type=MESH,
        ).start()

    def arrived(slot):
        pltpu.make_async_copy(table_ref.at[slot], table_ref.at[slot], in_sem.at[slot]).wait()

    def query_arrived(slot):
        pltpu.make_async_copy(all_ref.at[slot], all_ref.at[slot], query_in_sem.at[slot]).wait()

    def pick(target):
        def some(step, carry):
            base = pl.multiple_of(step * 16, 16)
            for k in range(16):
                row = wanted_ref[target * per_range + base + k]
                picked[target, pl.ds(base + k, 1), :] = rows_ref[pl.ds(row, 1), :]
            return carry

        lax.fori_loop(0, per_range // 16, some, 0)

    def give(step, carry):
        target = (own + step) % pass_count
        pick(target)
        send(picked.at[target], cent * pass_count + own, (cent, target))
        return carry

    lax.fori_loop(1, pass_count, give, 0)
    all_ref[cent] = queries_ref[...]
    for side in sides:
        send_query(cent, side)
    send_query(cent, twin)
    pick(own)
    table_ref[cent * pass_count + own] = picked[own]

    def forward(slot):
        for side in sides:
            send(table_ref.at[slot], slot, side)
        send(table_ref.at[slot], slot, twin)

    forward(cent * pass_count + own)

    def take(step, carry):
        slot = cent * pass_count + (own + pass_count - step) % pass_count
        arrived(slot)
        forward(slot)
        return carry

    lax.fori_loop(1, pass_count, take, 0)
    for s in range(1, pairs):
        other = (pair + pairs - s) % pairs * 2 + core
        query_arrived(other)
        send_query(other, twin)

        def cross(step, carry):
            slot = other * pass_count + (own + pass_count - step) % pass_count
            arrived(slot)
            send(table_ref.at[slot], slot, twin)
            return carry

        lax.fori_loop(0, pass_count, cross, 0)

    for k in range(pairs):
        other = k * 2 + 1 - core
        query_arrived(other)

        def last(step, carry):
            arrived(other * pass_count + step)
            return carry

        lax.fori_loop(0, pass_count, last, 0)
    sent = table_ref.at[pl.ds(0, cent_count * pass_count - 1)]
    pltpu.make_async_copy(sent, sent, out_sem).wait()
    sent = all_ref.at[pl.ds(0, cent_count - 1)]
    pltpu.make_async_copy(sent, sent, query_out_sem).wait()


def spread_rows(queries, centroids, wanted, cent_count, pass_count):
    per_range = wanted.shape[0] // pass_count
    width = centroids.shape[1]
    slots = cent_count * pass_count
    return pl.pallas_call(
        functools.partial(spread_kernel, pass_count, cent_count, per_range),
        out_shape=(
            jax.ShapeDtypeStruct((slots, per_range, width), jnp.float32),
            jax.ShapeDtypeStruct((cent_count,) + queries.shape, jnp.float32),
        ),
        in_specs=[
            pl.BlockSpec(memory_space=pltpu.SMEM),
            pl.BlockSpec(memory_space=pltpu.HBM),
            pl.BlockSpec(memory_space=pltpu.VMEM),
        ],
        out_specs=(pl.BlockSpec(memory_space=pltpu.VMEM), pl.BlockSpec(memory_space=pltpu.VMEM)),
        scratch_shapes=[
            pltpu.VMEM(centroids.shape, jnp.float32),
            pltpu.VMEM((pass_count, per_range, width), jnp.float32),
            pltpu.SemaphoreType.DMA,
            pltpu.SemaphoreType.DMA,
            pltpu.SemaphoreType.DMA((slots,)),
            pltpu.SemaphoreType.DMA,
            pltpu.SemaphoreType.DMA((cent_count,)),
        ],
        compiler_params=pltpu.CompilerParams(
            collective_id=0, has_side_effects=True, vmem_limit_bytes=51 * 2**20
        ),
    )(wanted, centroids, queries)


def finish_kernel(
    pass_count, cent_count, part_ref, mask_ref, every_ref, box, out_sem, in_sem, box_out_sem, box_in_sem
):
    cent, own = lax.axis_index("cent"), lax.axis_index("pass")
    across = [(cent + s) % cent_count for s in range(1, cent_count)]
    along = [(own + s) % pass_count for s in range(1, pass_count)]
    meet([(c, own) for c in across] + [(cent, p) for p in along])
    copies = []
    for k, c in enumerate(across):
        copy = pltpu.make_async_remote_copy(
            src_ref=part_ref.at[c],
            dst_ref=every_ref.at[cent],
            send_sem=out_sem.at[k],
            recv_sem=in_sem.at[k],
            device_id=(c, own),
            device_id_type=MESH,
        )
        copy.start()
        copies.append(copy)
    every_ref[cent] = part_ref[cent]
    for copy in copies:
        copy.wait()
    box[own] = jnp.where(mask_ref[...] > 0, every_ref[...], floor_value)
    copies = []
    for k, p in enumerate(along):
        copy = pltpu.make_async_remote_copy(
            src_ref=box.at[own],
            dst_ref=box.at[own],
            send_sem=box_out_sem.at[k],
            recv_sem=box_in_sem.at[k],
            device_id=(cent, p),
            device_id_type=MESH,
        )
        copy.start()
        copies.append(copy)
    for copy in copies:
        copy.wait()


def exchange(values, near, far):
    return jnp.maximum(values[near], values[far]), jnp.minimum(values[near], values[far])


def settle(values):
    gap = len(values) // 2
    while gap:
        for i in range(len(values)):
            if not i & gap:
                values[i], values[i + gap] = exchange(values, i, i + gap)
        gap //= 2
    return values


def descending(values):
    if len(values) == 1:
        return values
    half = len(values) // 2
    return settle(descending(values[:half]) + descending(values[half:])[::-1])


def merged(first, second):
    return settle([jnp.maximum(x, y) for x, y in zip(first, second[::-1])])


def top_kernel(keep, box_ref, top_ref):
    pass_count, cent_count, group, mine = box_ref.shape
    values = [box_ref[p, c] for p in range(pass_count) for c in range(cent_count)]
    runs = [descending(values[i : i + keep]) for i in range(0, len(values), keep)]
    best = runs[0]
    for run in runs[1:]:
        best = merged(best, run)
    gap = mine // 2
    while gap:
        if mine % 128 == 0:
            moved = [pltpu.roll(x, gap, 1) for x in best]
        else:
            moved = [jnp.concatenate([x[:, gap:], x[:, :gap]], axis=1) for x in best]
        best = merged(best, moved)
        gap //= 2
    place = lax.broadcasted_iota(jnp.int32, (group, mine), 1)
    out = best[0]
    for k in range(1, keep):
        out = jnp.where(place == k, best[k], out)
    top_ref[...] = out[:, :keep]


def largest(box):
    return pl.pallas_call(
        functools.partial(top_kernel, KTOP),
        out_shape=jax.ShapeDtypeStruct((box.shape[2], KTOP), jnp.float32),
        in_specs=[pl.BlockSpec(memory_space=pltpu.VMEM)],
        out_specs=pl.BlockSpec(memory_space=pltpu.VMEM),
    )(box)


def finish(parts, mask, pass_count):
    cent_count = parts.shape[0]
    return pl.pallas_call(
        functools.partial(finish_kernel, pass_count, cent_count),
        out_shape=(
            jax.ShapeDtypeStruct(parts.shape, jnp.float32),
            jax.ShapeDtypeStruct((pass_count,) + parts.shape, jnp.float32),
        ),
        in_specs=[pl.BlockSpec(memory_space=pltpu.VMEM)] * 2,
        out_specs=(pl.BlockSpec(memory_space=pltpu.VMEM), pl.BlockSpec(memory_space=pltpu.VMEM)),
        scratch_shapes=[
            pltpu.SemaphoreType.DMA((cent_count,)),
            pltpu.SemaphoreType.DMA((cent_count,)),
            pltpu.SemaphoreType.DMA((pass_count,)),
            pltpu.SemaphoreType.DMA((pass_count,)),
        ],
        compiler_params=pltpu.CompilerParams(collective_id=1, has_side_effects=True),
    )(parts, mask)


def score_kernel(
    passage_len, where_ref, codes_ref, bits_ref, weights_ref, query_ref, fold_ref, table_ref, out_ref, held, best
):
    chunk = pl.program_id(0)
    width = weights_ref.shape[1]
    rows = passage_len * CHUNK
    words = width // 4
    per_tile = width // words

    def some(step, carry):
        base = pl.multiple_of(step * CHUNK, CHUNK)
        for k in range(CHUNK):
            code = codes_ref[chunk * rows + base + k]
            held[pl.ds(base + k, 1), :] = table_ref[pl.ds(code, 1), :]
        return carry

    lax.fori_loop(0, passage_len, some, 0, unroll=4)

    tiles = passage_len // per_tile
    packed = jnp.concatenate(
        [bits_ref[:, i * width : (i + 1) * width] for i in range(tiles)], axis=0
    )
    source = lax.broadcasted_iota(jnp.int32, (width, width * per_tile), 0)
    target = lax.broadcasted_iota(jnp.int32, (width, width * per_tile), 1)
    spread = jnp.where(target // 4 == source, 1.0, 0.0).astype(jnp.bfloat16)
    wide = jnp.dot(
        packed.astype(jnp.float32).astype(jnp.bfloat16), spread, preferred_element_type=jnp.float32
    ).astype(jnp.int32)
    shift = 2 * (lax.broadcasted_iota(jnp.int32, (1, width), 1) % 4)
    parts = []
    for a in range(per_tile):
        level = jnp.right_shift(wide[:, a * width : (a + 1) * width], shift) & 3
        value = jnp.where(
            level == 0,
            weights_ref[0:1, :],
            jnp.where(
                level == 1,
                weights_ref[1:2, :],
                jnp.where(level == 2, weights_ref[2:3, :], weights_ref[3:4, :]),
            ),
        )
        parts.append(value.reshape(tiles, 1, CHUNK, width))
    residual = jnp.concatenate(parts, axis=1).reshape(rows, width)
    token = (held[...] + residual).astype(jnp.bfloat16)
    token = jnp.concatenate([token, token], axis=1)
    score = jnp.dot(token, query_ref[...], preferred_element_type=jnp.float32)
    peak = jnp.max(score.reshape(passage_len, CHUNK, score.shape[1]), axis=0)
    best[pl.ds(pl.multiple_of(chunk * CHUNK, CHUNK), CHUNK), :] = peak

    @pl.when(chunk == pl.num_programs(0) - 1)
    def _():
        out_ref[...] = lax.dot_general(
            fold_ref[...],
            best[...],
            (((1,), (1,)), ((), ())),
            precision=lax.Precision.HIGHEST,
            preferred_element_type=jnp.float32,
        )


def score_passages(all_queries, table, codes, bits, weights, where, mine):
    query_count, query_len, width = all_queries.shape
    passage_len = codes.shape[0] // mine
    flat = all_queries.reshape(query_count * query_len, width)
    high = lax.reduce_precision(flat, 8, 7)
    both = jnp.concatenate([high, flat - high], axis=1).T.astype(jnp.bfloat16)
    fold = (
        jnp.arange(query_count * query_len)[None, :] // query_len == jnp.arange(query_count)[:, None]
    ).astype(jnp.float32)
    chunks = mine // CHUNK
    whole = pl.Buffered(buffer_count=1)
    return pl.pallas_call(
        functools.partial(score_kernel, passage_len),
        out_shape=jax.ShapeDtypeStruct((query_count, mine), jnp.float32),
        grid_spec=pltpu.PrefetchScalarGridSpec(
            num_scalar_prefetch=2,
            grid=(chunks,),
            in_specs=[
                pl.BlockSpec((CHUNK, bits.shape[1]), lambda c, w, k: (w[0] * chunks + c, 0)),
                pl.BlockSpec(weights.shape, lambda c, w, k: (0, 0)),
                pl.BlockSpec(both.shape, lambda c, w, k: (0, 0), pipeline_mode=whole),
                pl.BlockSpec(fold.shape, lambda c, w, k: (0, 0), pipeline_mode=whole),
                pl.BlockSpec(table.shape, lambda c, w, k: (0, 0), pipeline_mode=whole),
            ],
            out_specs=pl.BlockSpec((query_count, mine), lambda c, w, k: (0, 0)),
            scratch_shapes=[
                pltpu.VMEM((passage_len * CHUNK, width), jnp.float32),
                pltpu.VMEM((mine, query_count * query_len), jnp.float32),
            ],
        ),
        compiler_params=pltpu.CompilerParams(vmem_limit_bytes=48 * 2**20),
    )(where, codes, bits, weights, both, fold, table)


def body(
    queries,
    centroids,
    bucket_weights,
    touched,
    token_codes,
    residual_bits,
    candidate_blocks,
    block_counts,
):
    group_queries, query_len, width = queries.shape
    pass_count = lax.axis_size("pass")
    cent_count = lax.axis_size("cent")
    row_count = centroids.shape[0]
    cent = lax.axis_index("cent").astype(jnp.int32)
    per_range = touched.shape[1] // (pass_count * cent_count)
    owner = cent * pass_count + lax.axis_index("pass")
    wanted = lax.dynamic_slice_in_dim(touched, owner * per_range, per_range, 1) - owner * row_count
    table, all_queries = spread_rows(queries, centroids, wanted.reshape(-1), cent_count, pass_count)
    table = table.reshape(-1, width)
    all_queries = all_queries.reshape(-1, query_len, width)

    passages, passage_len = token_codes.shape
    mine = passages // cent_count
    codes = lax.dynamic_slice_in_dim(token_codes, cent * mine, mine, 0)
    codes = codes.reshape(mine // CHUNK, CHUNK, passage_len).transpose(0, 2, 1).reshape(-1)
    scored = score_passages(
        all_queries, table, codes, residual_bits, bucket_weights, cent.reshape(1), mine
    )

    blocks = candidate_blocks[:, 0, :]
    block_count = blocks.shape[1]
    stored = passages // BLK
    live = jnp.arange(block_count, dtype=jnp.int32)[None, :] < block_counts
    holds = blocks[:, :, None] == jnp.arange(stored, dtype=jnp.int32)[None, None, :]
    wanted_blocks = jnp.any(holds & live[:, :, None], axis=1).astype(jnp.int32)
    mask = jnp.repeat(wanted_blocks, BLK, axis=1).reshape(group_queries, cent_count, mine)
    parts = scored.reshape(cent_count, group_queries, mine)
    every, box = finish(parts, mask.transpose(1, 0, 2), pass_count)
    by_block = every.transpose(1, 0, 2).reshape(group_queries, 1, stored, BLK)
    slots = jnp.sum(jnp.where(holds[:, :, :, None], by_block, 0.0), axis=2)
    plain = jnp.where(live[:, :, None], slots, 0.0).reshape(group_queries, -1)
    return plain[:, None, :], largest(box)


def solution(mesh):
    placed = (
        P("cent", None, None),
        P(("cent", "pass"), None),
        P(),
        P(),
        P("pass", None),
        P("pass", None),
        P("cent", "pass", None),
        P("cent", "pass"),
    )
    return jax.shard_map(
        body,
        mesh=mesh,
        in_specs=placed,
        out_specs=(P("cent", "pass", None), P("cent", None)),
        check_vma=False,
    )
```

```python
import functools

import jax
import jax.numpy as jnp
from jax import lax
from jax.experimental import pallas as pl
from jax.experimental.pallas import tpu as pltpu
from jax.sharding import PartitionSpec as P

BLK = 16
KTOP = 32
CHUNK = 16

floor_value = -1e30


MESH = pl.DeviceIdType.MESH


def meet(peers):
    barrier = pltpu.get_barrier_semaphore()
    for peer in peers:
        pl.semaphore_signal(barrier, inc=1, device_id=peer, device_id_type=MESH)
    pl.semaphore_wait(barrier, len(peers))


def spread_kernel(
    pass_count,
    cent_count,
    per_range,
    wanted_ref,
    stored_ref,
    queries_ref,
    table_ref,
    all_ref,
    rows_ref,
    picked,
    fetch_sem,
    out_sem,
    in_sem,
    query_out_sem,
    query_in_sem,
):
    cent, own = lax.axis_index("cent"), lax.axis_index("pass")
    core, pair = cent % 2, cent // 2
    pairs = cent_count // 2
    twin = (cent + 1 - 2 * core, own)
    sides = [((pair + s) % pairs * 2 + core, own) for s in range(1, pairs)]
    fetch = pltpu.make_async_copy(stored_ref, rows_ref, fetch_sem)
    fetch.start()
    meet([(cent, (own + s) % pass_count) for s in range(1, pass_count)] + sides + [twin])
    fetch.wait()

    def send_query(slot, peer, source=None):
        pltpu.make_async_remote_copy(
            src_ref=all_ref.at[slot] if source is None else source,
            dst_ref=all_ref.at[slot],
            send_sem=query_out_sem,
            recv_sem=query_in_sem.at[slot],
            device_id=peer,
            device_id_type=MESH,
        ).start()

    def send(source, slot, peer):
        pltpu.make_async_remote_copy(
            src_ref=source,
            dst_ref=table_ref.at[slot],
            send_sem=out_sem,
            recv_sem=in_sem.at[slot],
            device_id=peer,
            device_id_type=MESH,
        ).start()

    def arrived(slot):
        pltpu.make_async_copy(table_ref.at[slot], table_ref.at[slot], in_sem.at[slot]).wait()

    def query_arrived(slot):
        pltpu.make_async_copy(all_ref.at[slot], all_ref.at[slot], query_in_sem.at[slot]).wait()

    def pick(target):
        def some(step, carry):
            base = pl.multiple_of(step * 16, 16)
            for k in range(16):
                row = wanted_ref[target * per_range + base + k]
                picked[target, pl.ds(base + k, 1), :] = rows_ref[pl.ds(row, 1), :]
            return carry

        lax.fori_loop(0, per_range // 16, some, 0)

    def forward(slot):
        for side in sides:
            send(table_ref.at[slot], slot, side)
        send(table_ref.at[slot], slot, twin)

    pick(own)
    table_ref[cent * pass_count + own] = picked[own]
    forward(cent * pass_count + own)

    def give(step, carry):
        target = (own + step) % pass_count
        pick(target)
        send(picked.at[target], cent * pass_count + own, (cent, target))
        return carry

    lax.fori_loop(1, pass_count, give, 0)
    all_ref[cent] = queries_ref[...]
    for side in sides:
        send_query(cent, side)
    send_query(cent, twin)

    def take(step, carry):
        slot = cent * pass_count + (own + pass_count - step) % pass_count
        arrived(slot)
        forward(slot)
        return carry

    lax.fori_loop(1, pass_count, take, 0)
    for s in range(1, pairs):
        other = (pair + pairs - s) % pairs * 2 + core
        query_arrived(other)
        send_query(other, twin)

        def cross(step, carry):
            slot = other * pass_count + (own + pass_count - step) % pass_count
            arrived(slot)
            send(table_ref.at[slot], slot, twin)
            return carry

        lax.fori_loop(0, pass_count, cross, 0)

    for k in range(pairs):
        other = k * 2 + 1 - core
        query_arrived(other)

        def last(step, carry):
            arrived(other * pass_count + step)
            return carry

        lax.fori_loop(0, pass_count, last, 0)
    sent = table_ref.at[pl.ds(0, cent_count * pass_count - 1)]
    pltpu.make_async_copy(sent, sent, out_sem).wait()
    sent = all_ref.at[pl.ds(0, cent_count - 1)]
    pltpu.make_async_copy(sent, sent, query_out_sem).wait()


def spread_rows(queries, centroids, wanted, cent_count, pass_count):
    per_range = wanted.shape[0] // pass_count
    width = centroids.shape[1]
    slots = cent_count * pass_count
    return pl.pallas_call(
        functools.partial(spread_kernel, pass_count, cent_count, per_range),
        out_shape=(
            jax.ShapeDtypeStruct((slots, per_range, width), jnp.float32),
            jax.ShapeDtypeStruct((cent_count,) + queries.shape, jnp.float32),
        ),
        in_specs=[
            pl.BlockSpec(memory_space=pltpu.SMEM),
            pl.BlockSpec(memory_space=pltpu.HBM),
            pl.BlockSpec(memory_space=pltpu.VMEM),
        ],
        out_specs=(pl.BlockSpec(memory_space=pltpu.VMEM), pl.BlockSpec(memory_space=pltpu.VMEM)),
        scratch_shapes=[
            pltpu.VMEM(centroids.shape, jnp.float32),
            pltpu.VMEM((pass_count, per_range, width), jnp.float32),
            pltpu.SemaphoreType.DMA,
            pltpu.SemaphoreType.DMA,
            pltpu.SemaphoreType.DMA((slots,)),
            pltpu.SemaphoreType.DMA,
            pltpu.SemaphoreType.DMA((cent_count,)),
        ],
        compiler_params=pltpu.CompilerParams(
            collective_id=0, has_side_effects=True, vmem_limit_bytes=51 * 2**20
        ),
    )(wanted, centroids, queries)


def finish_kernel(
    pass_count, cent_count, part_ref, mask_ref, every_ref, box, out_sem, in_sem, box_out_sem, box_in_sem
):
    cent, own = lax.axis_index("cent"), lax.axis_index("pass")
    across = [(cent + s) % cent_count for s in range(1, cent_count)]
    along = [(own + s) % pass_count for s in range(1, pass_count)]
    meet([(c, own) for c in across] + [(cent, p) for p in along])
    copies = []
    for k, c in enumerate(across):
        copy = pltpu.make_async_remote_copy(
            src_ref=part_ref.at[c],
            dst_ref=every_ref.at[cent],
            send_sem=out_sem.at[k],
            recv_sem=in_sem.at[k],
            device_id=(c, own),
            device_id_type=MESH,
        )
        copy.start()
        copies.append(copy)
    every_ref[cent] = part_ref[cent]
    for copy in copies:
        copy.wait()
    box[own] = jnp.where(mask_ref[...] > 0, every_ref[...], floor_value)
    copies = []
    for k, p in enumerate(along):
        copy = pltpu.make_async_remote_copy(
            src_ref=box.at[own],
            dst_ref=box.at[own],
            send_sem=box_out_sem.at[k],
            recv_sem=box_in_sem.at[k],
            device_id=(cent, p),
            device_id_type=MESH,
        )
        copy.start()
        copies.append(copy)
    for copy in copies:
        copy.wait()


def exchange(values, near, far):
    return jnp.maximum(values[near], values[far]), jnp.minimum(values[near], values[far])


def settle(values):
    gap = len(values) // 2
    while gap:
        for i in range(len(values)):
            if not i & gap:
                values[i], values[i + gap] = exchange(values, i, i + gap)
        gap //= 2
    return values


def descending(values):
    if len(values) == 1:
        return values
    half = len(values) // 2
    return settle(descending(values[:half]) + descending(values[half:])[::-1])


def merged(first, second):
    return settle([jnp.maximum(x, y) for x, y in zip(first, second[::-1])])


def top_kernel(keep, box_ref, top_ref):
    pass_count, cent_count, group, mine = box_ref.shape
    values = [box_ref[p, c] for p in range(pass_count) for c in range(cent_count)]
    runs = [descending(values[i : i + keep]) for i in range(0, len(values), keep)]
    best = runs[0]
    for run in runs[1:]:
        best = merged(best, run)
    gap = mine // 2
    while gap:
        if mine % 128 == 0:
            moved = [pltpu.roll(x, gap, 1) for x in best]
        else:
            moved = [jnp.concatenate([x[:, gap:], x[:, :gap]], axis=1) for x in best]
        best = merged(best, moved)
        gap //= 2
    place = lax.broadcasted_iota(jnp.int32, (group, mine), 1)
    out = best[0]
    for k in range(1, keep):
        out = jnp.where(place == k, best[k], out)
    top_ref[...] = out[:, :keep]


def largest(box):
    return pl.pallas_call(
        functools.partial(top_kernel, KTOP),
        out_shape=jax.ShapeDtypeStruct((box.shape[2], KTOP), jnp.float32),
        in_specs=[pl.BlockSpec(memory_space=pltpu.VMEM)],
        out_specs=pl.BlockSpec(memory_space=pltpu.VMEM),
    )(box)


def finish(parts, mask, pass_count):
    cent_count = parts.shape[0]
    return pl.pallas_call(
        functools.partial(finish_kernel, pass_count, cent_count),
        out_shape=(
            jax.ShapeDtypeStruct(parts.shape, jnp.float32),
            jax.ShapeDtypeStruct((pass_count,) + parts.shape, jnp.float32),
        ),
        in_specs=[pl.BlockSpec(memory_space=pltpu.VMEM)] * 2,
        out_specs=(pl.BlockSpec(memory_space=pltpu.VMEM), pl.BlockSpec(memory_space=pltpu.VMEM)),
        scratch_shapes=[
            pltpu.SemaphoreType.DMA((cent_count,)),
            pltpu.SemaphoreType.DMA((cent_count,)),
            pltpu.SemaphoreType.DMA((pass_count,)),
            pltpu.SemaphoreType.DMA((pass_count,)),
        ],
        compiler_params=pltpu.CompilerParams(collective_id=1, has_side_effects=True),
    )(parts, mask)


def score_kernel(
    passage_len, where_ref, codes_ref, bits_ref, weights_ref, query_ref, fold_ref, table_ref, out_ref, held, best
):
    chunk = pl.program_id(0)
    width = weights_ref.shape[1]
    rows = passage_len * CHUNK
    words = width // 4
    per_tile = width // words

    def some(step, carry):
        base = pl.multiple_of(step * CHUNK, CHUNK)
        for k in range(CHUNK):
            code = codes_ref[chunk * rows + base + k]
            held[pl.ds(base + k, 1), :] = table_ref[pl.ds(code, 1), :]
        return carry

    lax.fori_loop(0, passage_len, some, 0, unroll=4)

    tiles = passage_len // per_tile
    packed = jnp.concatenate(
        [bits_ref[:, i * width : (i + 1) * width] for i in range(tiles)], axis=0
    )
    source = lax.broadcasted_iota(jnp.int32, (width, width * per_tile), 0)
    target = lax.broadcasted_iota(jnp.int32, (width, width * per_tile), 1)
    spread = jnp.where(target // 4 == source, 1.0, 0.0).astype(jnp.bfloat16)
    wide = jnp.dot(
        packed.astype(jnp.float32).astype(jnp.bfloat16), spread, preferred_element_type=jnp.float32
    ).astype(jnp.int32)
    shift = 2 * (lax.broadcasted_iota(jnp.int32, (1, width), 1) % 4)
    parts = []
    for a in range(per_tile):
        level = jnp.right_shift(wide[:, a * width : (a + 1) * width], shift) & 3
        value = jnp.where(
            level == 0,
            weights_ref[0:1, :],
            jnp.where(
                level == 1,
                weights_ref[1:2, :],
                jnp.where(level == 2, weights_ref[2:3, :], weights_ref[3:4, :]),
            ),
        )
        parts.append(value.reshape(tiles, 1, CHUNK, width))
    residual = jnp.concatenate(parts, axis=1).reshape(rows, width)
    token = (held[...] + residual).astype(jnp.bfloat16)
    token = jnp.concatenate([token, token], axis=1)
    score = jnp.dot(token, query_ref[...], preferred_element_type=jnp.float32)
    peak = jnp.max(score.reshape(passage_len, CHUNK, score.shape[1]), axis=0)
    best[pl.ds(pl.multiple_of(chunk * CHUNK, CHUNK), CHUNK), :] = peak

    @pl.when(chunk == pl.num_programs(0) - 1)
    def _():
        out_ref[...] = lax.dot_general(
            fold_ref[...],
            best[...],
            (((1,), (1,)), ((), ())),
            precision=lax.Precision.HIGHEST,
            preferred_element_type=jnp.float32,
        )


def score_passages(all_queries, table, codes, bits, weights, where, mine):
    query_count, query_len, width = all_queries.shape
    passage_len = codes.shape[0] // mine
    flat = all_queries.reshape(query_count * query_len, width)
    high = lax.reduce_precision(flat, 8, 7)
    both = jnp.concatenate([high, flat - high], axis=1).T.astype(jnp.bfloat16)
    fold = (
        jnp.arange(query_count * query_len)[None, :] // query_len == jnp.arange(query_count)[:, None]
    ).astype(jnp.float32)
    chunks = mine // CHUNK
    whole = pl.Buffered(buffer_count=1)
    return pl.pallas_call(
        functools.partial(score_kernel, passage_len),
        out_shape=jax.ShapeDtypeStruct((query_count, mine), jnp.float32),
        grid_spec=pltpu.PrefetchScalarGridSpec(
            num_scalar_prefetch=2,
            grid=(chunks,),
            in_specs=[
                pl.BlockSpec((CHUNK, bits.shape[1]), lambda c, w, k: (w[0] * chunks + c, 0)),
                pl.BlockSpec(weights.shape, lambda c, w, k: (0, 0)),
                pl.BlockSpec(both.shape, lambda c, w, k: (0, 0), pipeline_mode=whole),
                pl.BlockSpec(fold.shape, lambda c, w, k: (0, 0), pipeline_mode=whole),
                pl.BlockSpec(table.shape, lambda c, w, k: (0, 0), pipeline_mode=whole),
            ],
            out_specs=pl.BlockSpec((query_count, mine), lambda c, w, k: (0, 0)),
            scratch_shapes=[
                pltpu.VMEM((passage_len * CHUNK, width), jnp.float32),
                pltpu.VMEM((mine, query_count * query_len), jnp.float32),
            ],
        ),
        compiler_params=pltpu.CompilerParams(vmem_limit_bytes=48 * 2**20),
    )(where, codes, bits, weights, both, fold, table)


def body(
    queries,
    centroids,
    bucket_weights,
    touched,
    token_codes,
    residual_bits,
    candidate_blocks,
    block_counts,
):
    group_queries, query_len, width = queries.shape
    pass_count = lax.axis_size("pass")
    cent_count = lax.axis_size("cent")
    row_count = centroids.shape[0]
    cent = lax.axis_index("cent").astype(jnp.int32)
    per_range = touched.shape[1] // (pass_count * cent_count)
    owner = cent * pass_count + lax.axis_index("pass")
    wanted = lax.dynamic_slice_in_dim(touched, owner * per_range, per_range, 1) - owner * row_count
    table, all_queries = spread_rows(queries, centroids, wanted.reshape(-1), cent_count, pass_count)
    table = table.reshape(-1, width)
    all_queries = all_queries.reshape(-1, query_len, width)

    passages, passage_len = token_codes.shape
    mine = passages // cent_count
    codes = lax.dynamic_slice_in_dim(token_codes, cent * mine, mine, 0)
    codes = codes.reshape(mine // CHUNK, CHUNK, passage_len).transpose(0, 2, 1).reshape(-1)
    scored = score_passages(
        all_queries, table, codes, residual_bits, bucket_weights, cent.reshape(1), mine
    )

    blocks = candidate_blocks[:, 0, :]
    block_count = blocks.shape[1]
    stored = passages // BLK
    live = jnp.arange(block_count, dtype=jnp.int32)[None, :] < block_counts
    holds = blocks[:, :, None] == jnp.arange(stored, dtype=jnp.int32)[None, None, :]
    wanted_blocks = jnp.any(holds & live[:, :, None], axis=1).astype(jnp.int32)
    mask = jnp.repeat(wanted_blocks, BLK, axis=1).reshape(group_queries, cent_count, mine)
    parts = scored.reshape(cent_count, group_queries, mine)
    every, box = finish(parts, mask.transpose(1, 0, 2), pass_count)
    by_block = every.transpose(1, 0, 2).reshape(group_queries, 1, stored, BLK)
    slots = jnp.sum(jnp.where(holds[:, :, :, None], by_block, 0.0), axis=2)
    plain = jnp.where(live[:, :, None], slots, 0.0).reshape(group_queries, -1)
    return plain[:, None, :], largest(box)


def solution(mesh):
    placed = (
        P("cent", None, None),
        P(("cent", "pass"), None),
        P(),
        P(),
        P("pass", None),
        P("pass", None),
        P("cent", "pass", None),
        P("cent", "pass"),
    )
    return jax.shard_map(
        body,
        mesh=mesh,
        in_specs=placed,
        out_specs=(P("cent", "pass", None), P("cent", None)),
        check_vma=False,
    )
```
